512 devices in a mesh: rows: 32 (over z_lo, x), cols: 16 (over y, z_hi, core).
Axes of the slice: x: 4, y: 4, z: 16 (z_hi: 2, z_lo: 8; z = z_hi * 8 + z_lo), core: 2. Of those that a mesh axis runs over, the one named last changes fastest.
Arguments:
- left_feat: bfloat16 [320, 32, 2048], P(None, 'rows', 'cols'), may hold values from -6 to 6
- right_feat: bfloat16 [320, 32, 2048], P(None, 'rows', 'cols'), may hold values from -6 to 6
- grad_out: bfloat16 [32, 48, 32, 2048], P(None, None, 'rows', 'cols'), may hold values from -6 to 6
- conv_weight: bfloat16 [32, 40, 3, 3, 3], replicated, may hold values from -0.21875 to 0.21875
Outputs:
- grad_left: bfloat16 [320, 32, 2048], P(None, 'rows', 'cols')
- grad_right: bfloat16 [320, 32, 2048], P(None, 'rows', 'cols')
- grad_weight: float32 [32, 40, 3, 3, 3], replicated
The draws below stay inside these ranges and needn't reach their ends.
All inputs are finite; a program needn't handle non-finite values.
Results may differ from the reference program's by a relative error of at most 0.0029.
Values may be sent and summed in bfloat16 or wider, within the bound.
A program may use at most 64 MiB of HBM per device.

```python
import math
import jax
import jax.numpy as jnp
from jax import lax

F = 320
G = 40
C_OUT = 32
D = 48
H_DEV = 1
W_DEV = 128
HH = 32
WW = 2048
N_ROWS = 32
N_COLS = 16


def level_of(key, dims, shards, least, largest):
    def one(position, parts):
        steps = jax.random.uniform(jax.random.fold_in(jax.random.fold_in(key, 6), position), (parts,), jnp.float32, least / len(shards), largest / len(shards))
        return jnp.repeat(jnp.exp(steps), dims[position] // parts).reshape((-1,) + (1,) * (len(dims) - position - 1))

    factor_of = one(*shards[0])
    for cut in shards[1:]:
        factor_of = factor_of * one(*cut)
    return factor_of


def centred(rng, shape, width, reach, shards=(), held_as=jnp.bfloat16):
    entries = width * jax.random.normal(rng, shape, jnp.float32)
    if shards:
        entries = entries * level_of(rng, shape, shards, -0.22, 0.18)
    return jnp.clip(entries, -reach, reach).astype(held_as)


def setup_inputs(seed: int = 0) -> dict:
    arg_keys = jax.random.split(jax.random.key(seed), 5)
    return {
        "left_feat": centred(arg_keys[0], (F, HH, WW), 1.0, 6.0, ((1, 32), (2, 16))),
        "right_feat": centred(arg_keys[1], (F, HH, WW), 1.0, 6.0, ((1, 32), (2, 16))),
        "grad_out": centred(arg_keys[2], (C_OUT, D, HH, WW), 1.0, 6.0, ((2, 32), (3, 16))),
        "conv_weight": centred(arg_keys[3], (C_OUT, G, 3, 3, 3), (C_OUT * 27) ** -0.5, 0.21875),
    }


def correlate(left_band, right_ext, levels, groups):
    channels, band_rows, tile_width = left_band.shape
    group_size = channels // groups
    left_wide = left_band.astype(jnp.float32)
    slabs = []
    for level in range(levels):
        shifted = right_ext[:, :, levels - 1 - level:levels - 1 - level + tile_width].astype(jnp.float32)
        product = (left_wide * shifted).reshape(groups, group_size, band_rows, tile_width)
        slabs.append(lax.optimization_barrier(jnp.sum(product, axis=1)) * (1.0 / group_size))
    return jnp.stack(slabs, axis=1)

def feature_grads(grad_volume, left_band, right_ext, levels, groups):
    channels, band_rows, tile_width = left_band.shape
    group_size = channels // groups
    left_wide = left_band.astype(jnp.float32).reshape(groups, group_size, band_rows, tile_width)
    grad_left = jnp.zeros((groups, group_size, band_rows, tile_width), jnp.float32)
    grad_ext = jnp.zeros((channels, band_rows, tile_width + levels - 1), jnp.float32)
    for level in range(levels):
        shifted = right_ext[:, :, levels - 1 - level:levels - 1 - level + tile_width].astype(jnp.float32)
        slab = grad_volume[:, level][:, None]
        grad_left = grad_left + slab * shifted.reshape(groups, group_size, band_rows, tile_width)
        spread = (slab * left_wide).reshape(channels, band_rows, tile_width)
        grad_ext = grad_ext + jnp.pad(spread, ((0, 0), (0, 0), (levels - 1 - level, level)))
    scale = 1.0 / group_size
    return (grad_left.reshape(channels, band_rows, tile_width) * scale, grad_ext * scale)

def reference(left_feat, right_feat, grad_out, conv_weight):
    levels = D
    groups = G
    band_rows = H_DEV
    full_width = W_DEV * N_COLS
    padded = jnp.pad(grad_out, ((0, 0), (1, 1), (1, 1), (1, 1)))
    weight_wide = conv_weight.astype(jnp.float32)

    def one_band(summed, band_index):
        first_row = (band_index * band_rows).astype(jnp.int32)
        left_band = lax.dynamic_slice_in_dim(left_feat, first_row, band_rows, 1)
        right_band = lax.dynamic_slice_in_dim(right_feat, first_row, band_rows, 1)
        right_ext = jnp.pad(right_band, ((0, 0), (0, 0), (levels - 1, 0)))
        volume = correlate(left_band, right_ext, levels, groups).astype(jnp.bfloat16)
        volume_wide = volume.astype(jnp.float32)
        padded_band = lax.dynamic_slice_in_dim(padded, first_row, band_rows + 2, 2).astype(jnp.float32)
        grad_volume = jnp.zeros((groups, levels, band_rows, full_width), jnp.float32)
        kernel_terms = []
        for along_d in range(3):
            for along_h in range(3):
                for along_w in range(3):
                    window_cut = padded_band[:, 2 - along_d:2 - along_d + levels, 2 - along_h:2 - along_h + band_rows, 2 - along_w:2 - along_w + full_width]
                    grad_volume = grad_volume + jnp.einsum('oi,odhw->idhw', weight_wide[:, :, along_d, along_h, along_w], window_cut)
                    kernel_terms.append(jnp.einsum('idhw,odhw->oi', volume_wide, window_cut))
        summed = summed + jnp.stack(kernel_terms, axis=-1).reshape(summed.shape)
        grad_left, grad_ext = feature_grads(grad_volume, left_band, right_ext, levels, groups)
        grad_right = grad_ext[:, :, levels - 1:]
        return (summed, (grad_left.astype(jnp.bfloat16), grad_right.astype(jnp.bfloat16)))
    start_total = jnp.zeros(conv_weight.shape, jnp.float32)
    summed, (left_bands, right_bands) = lax.scan(one_band, start_total, jnp.arange(N_ROWS, dtype=jnp.int32))
    channels = left_feat.shape[0]
    grad_left = jnp.transpose(left_bands, (1, 0, 2, 3)).reshape(channels, band_rows * N_ROWS, full_width)
    grad_right = jnp.transpose(right_bands, (1, 0, 2, 3)).reshape(channels, band_rows * N_ROWS, full_width)
    cells = levels * band_rows * N_ROWS * full_width
    grad_weight = summed * (1.0 / math.sqrt(cells))
    return (grad_left, grad_right, grad_weight)
```

```python
import functools
import math

import jax
import jax.numpy as jnp
from jax import lax
from jax.experimental import pallas as pl
from jax.experimental.pallas import tpu as pltpu
from jax.sharding import PartitionSpec as P

MESH = pl.DeviceIdType.MESH
F32, BF16 = jnp.float32, jnp.bfloat16
ROWS, COLS = 32, 16
D, G, O, C, LANES = 48, 40, 32, 320, 128
TAPS = 9 * O
PLANE, DEEP = 32, 16
CHUNKS, CHUNK = 18, 16
HALF = C // 2


def plane_device(q, z):
    row = lax.rem(z, 8) * 4 + lax.rem(lax.div(q, 2), 4)
    return (row, lax.div(q, 8) * 4 + lax.div(z, 8) * 2 + lax.rem(q, 2))


def chunk_owner(j):
    return jnp.where(j < 16, 2 * j, jnp.where(j == 16, 1, 17))


def kernel(
    left, right, cot, weight, out_left, out_right, out_weight,
    wide, above, below, window, volume, grad_vol, left32, right32, border32, gl32, gr32, spill32,
    edge_send, edges, border_send, border, spill_send, spill, mixed, weight_t, terms, total,
    part1, part2, s_row, r_row, s_edge, r_edge, s_one, r_one, s1, r1, s2, r2, s3, r3,
):
    row, col = lax.axis_index("rows"), lax.axis_index("cols")
    core = lax.rem(col, 2)
    q = (lax.div(col, 4) * 4 + lax.rem(row, 4)) * 2 + core
    z = lax.rem(lax.div(col, 2), 2) * 8 + lax.div(row, 4)
    is_owner = jnp.logical_or(core == 0, jnp.logical_or(q == 1, q == 17))
    mine = jnp.where(core == 0, lax.div(q, 2), jnp.where(q == 1, 16, 17))
    lane = lax.broadcasted_iota(jnp.int32, (8, LANES), 1)
    lane32 = lax.broadcasted_iota(jnp.int32, (O, LANES), 1)

    def inside(dr, dc):
        ok = None
        for pos, step, count in ((row, dr, ROWS), (col, dc, COLS)):
            if step:
                here = pos > 0 if step < 0 else pos < count - 1
                ok = here if ok is None else jnp.logical_and(ok, here)
        return ok

    around = [(dr, dc) for dr in (-1, 0, 1) for dc in (-1, 0, 1) if (dr, dc) != (0, 0)]

    gate = pltpu.get_barrier_semaphore()
    expected = PLANE + DEEP - 2

    def greet(device):
        pl.semaphore_signal(gate, inc=1, device_id=device, device_id_type=MESH)

    for dr, dc in around:
        ok = inside(dr, dc)
        expected = expected + ok.astype(jnp.int32)
        pl.when(ok)(functools.partial(greet, (row + dr, col + dc)))

    @pl.loop(0, PLANE)
    def _(p):
        pl.when(p != q)(functools.partial(greet, plane_device(p, z)))

    @pl.loop(0, DEEP)
    def _(p):
        pl.when(p != z)(functools.partial(greet, plane_device(q, p)))

    def widen(src, dst, rows, step):
        @pl.loop(0, rows // step)
        def _(i):
            part = pl.ds(pl.multiple_of(i * step, step), step)
            dst[part] = src[part].astype(F32)

    widen(right, right32, C, 64)
    low, high = right32[pl.ds(0, HALF)], right32[pl.ds(HALF, HALF)]
    lane_half = lax.broadcasted_iota(jnp.int32, (HALF, LANES), 1)
    border_send[...] = jnp.where(lane_half >= 64, low, pltpu.roll(high, 64, 1)).astype(BF16)
    widen(cot, wide, O * D, 64)

    def edge_body(d, carry):
        first, last = carry
        t = wide[pl.ds(d, O, stride=D), :]
        first = jnp.where(lane32 == d, pltpu.roll(t, d, 1), first)
        last = jnp.where(lane32 == d, pltpu.roll(t, d + 1, 1), last)
        return first, last

    blank = jnp.zeros((O, LANES), F32)
    first, last = lax.fori_loop(0, D, edge_body, (blank, blank), unroll=4)
    edge_send[0] = last.astype(BF16)
    edge_send[1] = first.astype(BF16)

    pl.semaphore_wait(gate, expected)

    def remote(src, dst, send, recv, device):
        return pltpu.make_async_remote_copy(src, dst, send, recv, device_id=device, device_id_type=MESH)

    border_copy = remote(border_send, border, s_one.at[0], r_one.at[0], (row, col + 1))
    pl.when(inside(0, 1))(border_copy.start)
    edge_copies = []
    for side, dc in ((0, 1), (1, -1)):
        for dr in (-1, 0, 1):
            copy = remote(
                edge_send.at[side], edges.at[side, dr + 1],
                s_edge.at[side, dr + 1], r_edge.at[side, dr + 1], (row + dr, col + dc),
            )
            pl.when(inside(dr, dc))(copy.start)
            edge_copies.append((copy, inside(dr, dc), inside(-dr, -dc), edges.at[side, dr + 1]))
    down_copy = remote(cot, above, s_row.at[0], r_row.at[0], (row + 1, col))
    up_copy = remote(cot, below, s_row.at[1], r_row.at[1], (row - 1, col))
    pl.when(inside(1, 0))(down_copy.start)
    pl.when(inside(-1, 0))(up_copy.start)

    widen(left, left32, C, 64)
    for ref in (volume, grad_vol):
        ref[pl.ds(0, G)] = jnp.zeros((G, LANES), F32)
        ref[pl.ds((D + 1) * G, G + 8)] = jnp.zeros((G + 8, LANES), F32)

    @pl.loop(0, D)
    def _(d):
        grad_vol[pl.ds(pl.multiple_of((d + 1) * G, 8), G)] = jnp.zeros((G, LANES), F32)

    mixed[...] = jnp.zeros_like(mixed)
    weight_t[...] = jnp.zeros_like(weight_t)
    for a in range(3):
        mixed[pl.ds(0, TAPS), pl.ds(0, G)] = weight[a].astype(F32)
        weight_t[pl.ds(a * G, G)] = jnp.transpose(mixed[...])[:G]
    weights = weight_t[...][:, :TAPS].astype(BF16)
    terms[...] = jnp.zeros_like(terms)

    def settle(copy, ok, ref):
        pl.when(ok)(copy.wait_recv)

        @pl.when(jnp.logical_not(ok))
        def _():
            ref[...] = jnp.zeros_like(ref)

    settle(border_copy, inside(0, -1), border)
    arrived = border[...].astype(F32)
    border32[pl.ds(0, HALF)] = arrived
    border32[pl.ds(HALF, HALF)] = pltpu.roll(arrived, 64, 1)

    def group_rows(ref, block, k):
        return ref[pl.ds(block * 64 + k, 8, stride=8), :]

    @pl.loop(0, G // 8)
    def _(block):
        own = [group_rows(right32, block, k) for k in range(8)]
        far = [group_rows(border32, block, k) for k in range(8)]
        lefts = [group_rows(left32, block, k) for k in range(8)]

        def level(d, carry):
            inner = lane < LANES - d
            total_ = None
            for k in range(8):
                shifted = pltpu.roll(jnp.where(inner, own[k], far[k]), d, 1)
                product = lefts[k] * shifted
                total_ = product if total_ is None else total_ + product
            volume[pl.ds(pl.multiple_of((d + 1) * G + block * 8, 8), 8)] = total_ * 0.125
            return carry

        lax.fori_loop(0, D, level, 0, unroll=4)

    def windows(b):
        from_left, from_right = edges[0, b].astype(F32), edges[1, b].astype(F32)

        def body(d, carry):
            t = wide[pl.ds(d, O, stride=D), :]
            after = jnp.where(lane32 == 127, pltpu.roll(from_right, 127 - d, 1), pltpu.roll(t, 127, 1))
            before = jnp.where(lane32 == 0, pltpu.roll(from_left, lax.rem(LANES - d, LANES), 1), pltpu.roll(t, 1, 1))
            base = d * TAPS + b * 96
            window[pl.ds(pl.multiple_of(base, 32), O)] = after.astype(BF16)
            window[pl.ds(pl.multiple_of(base + 32, 32), O)] = t.astype(BF16)
            window[pl.ds(pl.multiple_of(base + 64, 32), O)] = before.astype(BF16)
            return carry

        lax.fori_loop(0, D, body, 0, unroll=2)

    for copy, _, ok, ref in edge_copies:
        settle(copy, ok, ref)
    windows(1)
    settle(down_copy, inside(-1, 0), above)
    widen(above, wide, O * D, 64)
    windows(2)
    settle(up_copy, inside(1, 0), below)
    widen(below, wide, O * D, 64)
    windows(0)

    def block_of(d):
        return window[pl.ds(pl.multiple_of(d * TAPS, 32), TAPS)]

    def term_body(t, carry):
        lhs = jnp.concatenate([block_of(t * 4 + s) for s in range(4)], axis=1)
        rhs = jnp.concatenate(
            [volume[pl.ds(pl.multiple_of((t * 4 + s) * G, 8), LANES)].astype(BF16) for s in range(4)], axis=1
        )
        terms[...] += lax.dot_general(lhs, rhs, (((1,), (1,)), ((), ())), preferred_element_type=F32)
        return carry

    lax.fori_loop(0, D // 4, term_body, 0)

    def scatter(j, slot, p):
        return remote(terms.at[pl.ds(pl.multiple_of(j * CHUNK, CHUNK), CHUNK)], part1.at[slot], s1.at[j], r1.at[slot], plane_device(p, z))

    def across(slot, p):
        return remote(part2.at[z], part2.at[slot], s2.at[p], r2.at[slot], plane_device(q, p))

    def spread(j, p):
        part = total.at[pl.ds(pl.multiple_of(j * CHUNK, CHUNK), CHUNK)]
        return remote(part, part, s3.at[p], r3.at[j], plane_device(p, z))

    def others(count, me, what):
        @pl.loop(0, count)
        def _(p):
            pl.when(p != me)(lambda: what(p))

    def chunks(what):
        @pl.loop(0, CHUNKS)
        def _(j):
            p = chunk_owner(j)
            pl.when(p != q)(lambda: what(j, p))

    chunks(lambda j, p: scatter(j, q, p).start())

    def volume_body(t, carry):
        rhs = jnp.concatenate([block_of(t * 2), block_of(t * 2 + 1)], axis=1)
        spread_ = jnp.dot(weights, rhs, preferred_element_type=F32)
        for s in range(2):
            part = pl.ds(pl.multiple_of((t * 2 + s) * G, 8), 3 * G)
            grad_vol[part] += spread_[: 3 * G, s * LANES : (s + 1) * LANES]
        return carry

    lax.fori_loop(0, D // 2, volume_body, 0, unroll=2)

    @pl.when(is_owner)
    def _():
        others(PLANE, q, lambda p: scatter(0, p, p).wait_recv())
        part1[q] = terms[pl.ds(pl.multiple_of(mine * CHUNK, CHUNK), CHUNK)]
        partial = part1[0]
        for p in range(1, PLANE):
            partial = partial + part1[p]
        part2[z] = partial
        others(DEEP, z, lambda p: across(z, p).start())

    @pl.loop(0, G // 8)
    def _(block):
        own = [group_rows(right32, block, k) for k in range(8)]
        far = [group_rows(border32, block, k) for k in range(8)]
        lefts = [group_rows(left32, block, k) for k in range(8)]

        def level(d, carry):
            gl, gr, sp = carry
            inner = lane < LANES - d
            slab = grad_vol[pl.ds(pl.multiple_of((d + 1) * G + block * 8, 8), 8)]
            back = lax.rem(LANES - d, LANES)
            moved = pltpu.roll(slab, back, 1)
            here, there = jnp.where(inner, moved, 0.0), jnp.where(inner, 0.0, moved)
            gl = [gl[k] + slab * pltpu.roll(jnp.where(inner, own[k], far[k]), d, 1) for k in range(8)]
            turned = [pltpu.roll(lefts[k], back, 1) for k in range(8)]
            gr = [gr[k] + here * turned[k] for k in range(8)]
            sp = [sp[k] + there * turned[k] for k in range(8)]
            return gl, gr, sp

        zeros = [jnp.zeros((8, LANES), F32)] * 8
        gl, gr, sp = lax.fori_loop(0, D, level, (zeros, zeros, zeros), unroll=2)
        for k in range(8):
            part = pl.ds(block * 64 + k, 8, stride=8)
            gl32[part, :] = gl[k] * 0.125
            gr32[part, :] = gr[k] * 0.125
            spill32[part, :] = sp[k] * 0.125

    spill_send[...] = jnp.where(lane_half >= 64, spill32[pl.ds(0, HALF)], pltpu.roll(spill32[pl.ds(HALF, HALF)], 64, 1))
    spill_copy = remote(spill_send, spill, s_one.at[1], r_one.at[1], (row, col - 1))
    pl.when(inside(0, -1))(spill_copy.start)

    @pl.when(is_owner)
    def _():
        others(DEEP, z, lambda p: across(p, p).wait_recv())
        whole = part2[0]
        for p in range(1, DEEP):
            whole = whole + part2[p]
        total[pl.ds(pl.multiple_of(mine * CHUNK, CHUNK), CHUNK)] = whole
        others(PLANE, q, lambda p: spread(mine, p).start())

    out_left[...] = gl32[...].astype(BF16)
    settle(spill_copy, inside(0, 1), spill)
    extra = spill[...]
    upper = lane_half >= LANES - (D - 1)
    out_right[pl.ds(0, HALF)] = (gr32[pl.ds(0, HALF)] + jnp.where(upper, extra, 0.0)).astype(BF16)
    out_right[pl.ds(HALF, HALF)] = (
        gr32[pl.ds(HALF, HALF)] + jnp.where(upper, pltpu.roll(extra, 64, 1), 0.0)
    ).astype(BF16)

    chunks(lambda j, p: spread(j, p).wait_recv())
    scale = 1.0 / math.sqrt(D * ROWS * COLS * LANES)
    summed = total[...] * scale
    for a in range(3):
        turned = summed if a == 0 else pltpu.roll(summed, LANES - a * G, 1)
        out_weight[pl.ds(a * TAPS, TAPS)] = turned[:, :G]

    pl.when(inside(0, 1))(border_copy.wait_send)
    for copy, ok, _, _ in edge_copies:
        pl.when(ok)(copy.wait_send)
    pl.when(inside(1, 0))(down_copy.wait_send)
    pl.when(inside(-1, 0))(up_copy.wait_send)
    pl.when(inside(0, -1))(spill_copy.wait_send)
    chunks(lambda j, p: scatter(j, q, p).wait_send())

    @pl.when(is_owner)
    def _():
        others(DEEP, z, lambda p: across(z, p).wait_send())
        others(PLANE, q, lambda p: spread(mine, p).wait_send())


def shards(left_feat, right_feat, grad_out, conv_weight):
    vmem = pl.BlockSpec(memory_space=pltpu.VMEM)
    dma = pltpu.SemaphoreType.DMA
    weight = jnp.transpose(conv_weight, (2, 3, 4, 0, 1)).reshape(3, TAPS, G)
    padded = (D + 2) * G + 8
    wide_rows = lambda rows: pltpu.VMEM((rows, LANES), F32)
    half_rows = lambda rows: pltpu.VMEM((rows, LANES), BF16)
    grad_left, grad_right, grad_weight = pl.pallas_call(
        kernel,
        out_shape=(
            jax.ShapeDtypeStruct((C, LANES), BF16),
            jax.ShapeDtypeStruct((C, LANES), BF16),
            jax.ShapeDtypeStruct((3 * TAPS, G), F32),
        ),
        in_specs=[vmem] * 4,
        out_specs=(vmem,) * 3,
        scratch_shapes=[
            wide_rows(O * D), half_rows(O * D), half_rows(O * D), half_rows(D * TAPS),
            wide_rows(padded), wide_rows(padded),
            wide_rows(C), wide_rows(C), wide_rows(C), wide_rows(C), wide_rows(C), wide_rows(C),
            pltpu.VMEM((2, O, LANES), BF16), pltpu.VMEM((2, 3, O, LANES), BF16),
            half_rows(HALF), half_rows(HALF), wide_rows(HALF), wide_rows(HALF),
            wide_rows(384), pltpu.VMEM((LANES, 384), F32), wide_rows(TAPS), wide_rows(TAPS),
            pltpu.VMEM((PLANE, CHUNK, LANES), F32), pltpu.VMEM((DEEP, CHUNK, LANES), F32),
            dma((2,)), dma((2,)), dma((2, 3)), dma((2, 3)), dma((2,)), dma((2,)),
            dma((CHUNKS,)), dma((PLANE,)), dma((DEEP,)), dma((DEEP,)), dma((PLANE,)), dma((CHUNKS,)),
        ],
        compiler_params=pltpu.CompilerParams(
            collective_id=0, has_side_effects=True, vmem_limit_bytes=40 * 1024 * 1024
        ),
        cost_estimate=pl.CostEstimate(flops=10**9, bytes_accessed=4 * 10**6, transcendentals=0),
    )(
        left_feat.reshape(C, LANES),
        right_feat.reshape(C, LANES),
        grad_out.reshape(O * D, LANES),
        weight,
    )
    return (
        grad_left.reshape(C, 1, LANES),
        grad_right.reshape(C, 1, LANES),
        jnp.transpose(grad_weight.reshape(3, 3, 3, O, G), (3, 4, 0, 1, 2)),
    )


def solution(mesh):
    placed = (P(None, "rows", "cols"), P(None, "rows", "cols"), P(None, None, "rows", "cols"), P())
    return jax.shard_map(
        shards,
        mesh=mesh,
        in_specs=placed,
        out_specs=(P(None, "rows", "cols"), P(None, "rows", "cols"), P()),
        check_vma=False,
    )
```

```python
import functools
import math

import jax
import jax.numpy as jnp
from jax import lax
from jax.experimental import pallas as pl
from jax.experimental.pallas import tpu as pltpu
from jax.sharding import PartitionSpec as P

MESH = pl.DeviceIdType.MESH
F32, BF16 = jnp.float32, jnp.bfloat16
ROWS, COLS = 32, 16
D, G, O, C, LANES = 48, 40, 32, 320, 128
TAPS = 9 * O
PLANE, DEEP = 32, 16
CHUNKS, CHUNK = 18, 16
HALF = C // 2


def plane_device(q, z):
    row = lax.rem(z, 8) * 4 + lax.rem(lax.div(q, 2), 4)
    return (row, lax.div(q, 8) * 4 + lax.div(z, 8) * 2 + lax.rem(q, 2))


def chunk_owner(j):
    return jnp.where(j < 16, 2 * j, jnp.where(j == 16, 1, 17))


def kernel(
    left_in, right_in, cot_in, weight_in, out_left, out_right, out_weight,
    left, right, cot, weight, wide, above, below, window, volume, grad_vol, left32, right32, gl32, gr32, spill32,
    by_tap, by_tap_bf, ext, moved_right, moved_left, near, edge32, edge_send, edges, border_send, border,
    spill_send, spill, mixed, weight_t, terms, total,
    part1, part2, s_in, s_row, r_row, s_edge, r_edge, s_one, r_one, s1, r1, s2, r2, s3, r3,
):
    row, col = lax.axis_index("rows"), lax.axis_index("cols")
    core = lax.rem(col, 2)
    q = (lax.div(col, 4) * 4 + lax.rem(row, 4)) * 2 + core
    z = lax.rem(lax.div(col, 2), 2) * 8 + lax.div(row, 4)
    is_owner = jnp.logical_or(core == 0, jnp.logical_or(q == 1, q == 17))
    mine = jnp.where(core == 0, lax.div(q, 2), jnp.where(q == 1, 16, 17))
    lane = lax.broadcasted_iota(jnp.int32, (8, LANES), 1)
    lane32 = lax.broadcasted_iota(jnp.int32, (O, LANES), 1)

    def inside(dr, dc):
        ok = None
        for pos, step, count in ((row, dr, ROWS), (col, dc, COLS)):
            if step:
                here = pos > 0 if step < 0 else pos < count - 1
                ok = here if ok is None else jnp.logical_and(ok, here)
        return ok

    around = [(dr, dc) for dr in (-1, 0, 1) for dc in (-1, 0, 1) if (dr, dc) != (0, 0)]

    gate = pltpu.get_barrier_semaphore()
    expected = PLANE + DEEP - 2

    def greet(device):
        pl.semaphore_signal(gate, inc=1, device_id=device, device_id_type=MESH)

    for dr, dc in around:
        ok = inside(dr, dc)
        expected = expected + ok.astype(jnp.int32)
        pl.when(ok)(functools.partial(greet, (row + dr, col + dc)))

    @pl.loop(0, PLANE)
    def _(p):
        pl.when(p != q)(functools.partial(greet, plane_device(p, z)))

    @pl.loop(0, DEEP)
    def _(p):
        pl.when(p != z)(functools.partial(greet, plane_device(q, p)))

    loads = [
        pltpu.make_async_copy(src, dst, s_in.at[i])
        for i, (src, dst) in enumerate(((right_in, right), (cot_in, cot), (left_in, left), (weight_in, weight)))
    ]
    for load in loads:
        load.start()

    def widen(src, dst, rows, step):
        @pl.loop(0, rows // step)
        def _(i):
            part = pl.ds(pl.multiple_of(i * step, step), step)
            dst[part] = src[part].astype(F32)

    loads[0].wait()
    widen(right, right32, C, 64)
    low, high = right32[pl.ds(0, HALF)], right32[pl.ds(HALF, HALF)]
    lane_half = lax.broadcasted_iota(jnp.int32, (HALF, LANES), 1)
    border_send[...] = jnp.where(lane_half >= 64, low, pltpu.roll(high, 64, 1)).astype(BF16)
    loads[1].wait()
    widen(cot, wide, O * D, 64)

    def edge_body(d, carry):
        first, last = carry
        t = wide[pl.ds(d, O, stride=D), :]
        first = jnp.where(lane32 == d, pltpu.roll(t, d, 1), first)
        last = jnp.where(lane32 == d, pltpu.roll(t, d + 1, 1), last)
        return first, last

    blank = jnp.zeros((O, LANES), F32)
    first, last = lax.fori_loop(0, D, edge_body, (blank, blank), unroll=4)
    edge_send[0] = last.astype(BF16)
    edge_send[1] = first.astype(BF16)

    pl.semaphore_wait(gate, expected)

    def remote(src, dst, send, recv, device):
        return pltpu.make_async_remote_copy(src, dst, send, recv, device_id=device, device_id_type=MESH)

    border_copy = remote(border_send, border, s_one.at[0], r_one.at[0], (row, col + 1))
    pl.when(inside(0, 1))(border_copy.start)
    edge_copies = []
    for side, dc in ((0, 1), (1, -1)):
        for dr in (-1, 0, 1):
            copy = remote(
                edge_send.at[side], edges.at[side, dr + 1],
                s_edge.at[side, dr + 1], r_edge.at[side, dr + 1], (row + dr, col + dc),
            )
            pl.when(inside(dr, dc))(copy.start)
            edge_copies.append((copy, inside(dr, dc), inside(-dr, -dc), edges.at[side, dr + 1]))
    down_copy = remote(cot_in, above, s_row.at[0], r_row.at[0], (row + 1, col))
    up_copy = remote(cot_in, below, s_row.at[1], r_row.at[1], (row - 1, col))
    pl.when(inside(1, 0))(down_copy.start)
    pl.when(inside(-1, 0))(up_copy.start)

    loads[2].wait()
    loads[3].wait()
    widen(left, left32, C, 64)
    for ref in (volume, grad_vol):
        ref[pl.ds(0, G)] = jnp.zeros((G, LANES), F32)
        ref[pl.ds((D + 1) * G, G + 8)] = jnp.zeros((G + 8, LANES), F32)

    @pl.loop(0, D)
    def _(d):
        grad_vol[pl.ds(pl.multiple_of((d + 1) * G, 8), G)] = jnp.zeros((G, LANES), F32)

    mixed[...] = jnp.zeros_like(mixed)
    weight_t[...] = jnp.zeros_like(weight_t)
    for a in range(3):
        for b in range(3):
            for c in range(3):
                mixed[pl.ds(c * 96 + b * O, O), pl.ds(0, G)] = weight[a, pl.ds((b * 3 + c) * O, O), :].astype(F32)
        weight_t[pl.ds(a * G, G)] = jnp.transpose(mixed[...])[:G]
    weights = weight_t[...][:, :TAPS].astype(BF16)
    terms[...] = jnp.zeros_like(terms)

    def settle(copy, ok, ref):
        pl.when(ok)(copy.wait_recv)

        @pl.when(jnp.logical_not(ok))
        def _():
            ref[...] = jnp.zeros_like(ref)

    def regroup(ref):
        return jnp.concatenate([ref[pl.ds(k, G, stride=8), :] for k in range(8)], axis=0)

    by_tap[...] = regroup(left32)
    by_tap_bf[...] = by_tap[...].astype(BF16)
    ext[:, pl.ds(LANES, LANES)] = regroup(right32).astype(BF16)
    source = lax.broadcasted_iota(jnp.int32, (2 * LANES, LANES), 0) - lax.broadcasted_iota(jnp.int32, (2 * LANES, LANES), 1)
    ring = source[:LANES]

    def pick(hit):
        return jnp.where(hit, 1.0, 0.0).astype(BF16)

    def turn_body(t, carry):
        d = t * 2
        rule = jnp.concatenate([pick(jnp.logical_or(ring == d + s, ring == d + s - LANES)) for s in range(2)], axis=1)
        turned = jnp.dot(by_tap_bf[...], rule, preferred_element_type=F32)
        for s in range(2):
            moved_left[pl.ds(pl.multiple_of((d + s) * C, 8), C)] = turned[:, s * LANES : (s + 1) * LANES]
        return carry

    lax.fori_loop(0, D // 2, turn_body, 0, unroll=8)

    def centre(b):
        def body(d, carry):
            base = pl.multiple_of(d * TAPS + 96 + b * O, 32)
            window[pl.ds(base, O)] = wide[pl.ds(d, O, stride=D), :].astype(BF16)
            return carry

        lax.fori_loop(0, D, body, 0, unroll=4)

    centre(1)
    for copy, _, ok, ref in edge_copies:
        settle(copy, ok, ref)
    for b in range(3):
        from_left, from_right = edges[0, b].astype(F32), edges[1, b].astype(F32)
        edge32[pl.ds(b * O, O)] = jnp.where(lane32 < 64, from_left, pltpu.roll(from_right, 64, 1))
    row_j = lax.broadcasted_iota(jnp.int32, (LANES, LANES), 0)
    col_w = lax.broadcasted_iota(jnp.int32, (LANES, LANES), 1)
    near[pl.ds(0, LANES), pl.ds(0, LANES)] = pick(row_j == col_w + 1)
    near[pl.ds(0, LANES), pl.ds(LANES, LANES)] = pick(row_j == col_w - 1)
    near[pl.ds(LANES, LANES), pl.ds(0, LANES)] = pick(jnp.logical_and(row_j >= 64, col_w == LANES - 1))
    near[pl.ds(LANES, LANES), pl.ds(LANES, LANES)] = pick(jnp.logical_and(row_j < 64, col_w == 0))
    lane96 = lax.broadcasted_iota(jnp.int32, (96, LANES), 1)

    def windows_body(t, carry):
        rows = []
        for s in range(4):
            d = t * 4 + s
            hit = jnp.logical_or(lane96 == d, lane96 == d + 64)
            rim = jnp.where(hit, edge32[...], 0.0).astype(BF16)
            rows.append(jnp.concatenate([window[pl.ds(pl.multiple_of(d * TAPS + 96, 32), 96)], rim], axis=1))
        sides = jnp.dot(jnp.concatenate(rows, axis=0), near[...], preferred_element_type=F32).astype(BF16)
        for s in range(4):
            d = t * 4 + s
            window[pl.ds(pl.multiple_of(d * TAPS, 32), 96)] = sides[s * 96 : (s + 1) * 96, :LANES]
            window[pl.ds(pl.multiple_of(d * TAPS + 192, 32), 96)] = sides[s * 96 : (s + 1) * 96, LANES:]
        return carry

    def rows_part():
        pl.when(inside(-1, 0))(down_copy.wait_recv)
        widen(above, wide, O * D, 64)
        centre(2)
        pl.when(inside(1, 0))(up_copy.wait_recv)
        widen(below, wide, O * D, 64)
        centre(0)
        lax.fori_loop(0, D // 4, windows_body, 0)

    @pl.when(row == 0)
    def _():
        above[...] = jnp.zeros_like(above)

    @pl.when(row == ROWS - 1)
    def _():
        below[...] = jnp.zeros_like(below)

    late = z >= 4
    pl.when(late)(rows_part)

    settle(border_copy, inside(0, -1), border)
    arrived = border[...].astype(F32)
    right32[pl.ds(0, HALF)] = arrived
    right32[pl.ds(HALF, HALF)] = pltpu.roll(arrived, 64, 1)
    ext[:, pl.ds(0, LANES)] = regroup(right32).astype(BF16)

    def volume_pair(t, carry):
        d = t * 2
        rule = jnp.concatenate([pick(source == LANES - d - s) for s in range(2)], axis=1)
        moved = jnp.dot(ext[...], rule, preferred_element_type=F32)
        for s in range(2):
            part = moved[:, s * LANES : (s + 1) * LANES]
            moved_right[pl.ds(pl.multiple_of((d + s) * C, 8), C)] = part
            slab = by_tap[pl.ds(0, G)] * part[:G]
            for k in range(1, 8):
                slab = slab + by_tap[pl.ds(k * G, G)] * part[k * G : (k + 1) * G]
            volume[pl.ds(pl.multiple_of((d + s + 1) * G, 8), G)] = slab * 0.125
        return carry

    lax.fori_loop(0, D // 2, volume_pair, 0, unroll=8)
    pl.when(jnp.logical_not(late))(rows_part)

    def block_of(d):
        return window[pl.ds(pl.multiple_of(d * TAPS, 32), TAPS)]

    def term_body(t, carry):
        lhs = jnp.concatenate([block_of(t * 4 + s) for s in range(4)], axis=1)
        rhs = jnp.concatenate(
            [volume[pl.ds(pl.multiple_of((t * 4 + s) * G, 8), LANES)].astype(BF16) for s in range(4)], axis=1
        )
        terms[...] += lax.dot_general(lhs, rhs, (((1,), (1,)), ((), ())), preferred_element_type=F32)
        return carry

    lax.fori_loop(0, D // 4, term_body, 0, unroll=6)

    def scatter(j, slot, p):
        return remote(terms.at[pl.ds(pl.multiple_of(j * CHUNK, CHUNK), CHUNK)], part1.at[slot], s1.at[j], r1.at[slot], plane_device(p, z))

    def across(slot, p):
        return remote(part2.at[z], part2.at[slot], s2.at[p], r2.at[slot], plane_device(q, p))

    def spread(j, p):
        part = total.at[pl.ds(pl.multiple_of(j * CHUNK, CHUNK), CHUNK)]
        return remote(part, part, s3.at[p], r3.at[j], plane_device(p, z))

    def others(count, me, what):
        @pl.loop(0, count)
        def _(p):
            pl.when(p != me)(lambda: what(p))

    def chunks(what):
        @pl.loop(0, CHUNKS)
        def _(j):
            p = chunk_owner(j)
            pl.when(p != q)(lambda: what(j, p))

    chunks(lambda j, p: scatter(j, q, p).start())

    def volume_body(t, carry):
        rhs = jnp.concatenate([block_of(t * 2), block_of(t * 2 + 1)], axis=1)
        spread_ = jnp.dot(weights, rhs, preferred_element_type=F32)
        for s in range(2):
            part = pl.ds(pl.multiple_of((t * 2 + s) * G, 8), 3 * G)
            grad_vol[part] += spread_[: 3 * G, s * LANES : (s + 1) * LANES]
        return carry

    lax.fori_loop(0, D // 2, volume_body, 0, unroll=8)

    @pl.when(is_owner)
    def _():
        others(PLANE, q, lambda p: scatter(0, p, p).wait_recv())
        part1[q] = terms[pl.ds(pl.multiple_of(mine * CHUNK, CHUNK), CHUNK)]
        partial = part1[0]
        for p in range(1, PLANE):
            partial = partial + part1[p]
        part2[z] = partial
        others(DEEP, z, lambda p: across(z, p).start())

    @pl.loop(0, G // 8)
    def _(block):
        def level(d, carry):
            gl, gr, sp = carry
            inner = lane < LANES - d
            slab = grad_vol[pl.ds(pl.multiple_of((d + 1) * G + block * 8, 8), 8)]
            moved = pltpu.roll(slab, lax.rem(LANES - d, LANES), 1)
            here, there = jnp.where(inner, moved, 0.0), jnp.where(inner, 0.0, moved)
            at = [pl.ds(pl.multiple_of(d * C + k * G + block * 8, 8), 8) for k in range(8)]
            gl = [gl[k] + slab * moved_right[at[k]] for k in range(8)]
            turned = [moved_left[at[k]] for k in range(8)]
            gr = [gr[k] + here * turned[k] for k in range(8)]
            sp = [sp[k] + there * turned[k] for k in range(8)]
            return gl, gr, sp

        zeros = [jnp.zeros((8, LANES), F32)] * 8
        gl, gr, sp = lax.fori_loop(0, D, level, (zeros, zeros, zeros), unroll=16)
        for k in range(8):
            part = pl.ds(block * 64 + k, 8, stride=8)
            gl32[part, :] = gl[k] * 0.125
            gr32[part, :] = gr[k] * 0.125
            spill32[part, :] = sp[k] * 0.125

    spill_send[...] = jnp.where(lane_half >= 64, spill32[pl.ds(0, HALF)], pltpu.roll(spill32[pl.ds(HALF, HALF)], 64, 1))
    spill_copy = remote(spill_send, spill, s_one.at[1], r_one.at[1], (row, col - 1))
    pl.when(inside(0, -1))(spill_copy.start)

    @pl.when(is_owner)
    def _():
        others(DEEP, z, lambda p: across(p, p).wait_recv())
        whole = part2[0]
        for p in range(1, DEEP):
            whole = whole + part2[p]
        total[pl.ds(pl.multiple_of(mine * CHUNK, CHUNK), CHUNK)] = whole
        others(PLANE, q, lambda p: spread(mine, p).start())

    out_left[...] = gl32[...].astype(BF16)
    settle(spill_copy, inside(0, 1), spill)
    extra = spill[...]
    upper = lane_half >= LANES - (D - 1)
    out_right[pl.ds(0, HALF)] = (gr32[pl.ds(0, HALF)] + jnp.where(upper, extra, 0.0)).astype(BF16)
    out_right[pl.ds(HALF, HALF)] = (
        gr32[pl.ds(HALF, HALF)] + jnp.where(upper, pltpu.roll(extra, 64, 1), 0.0)
    ).astype(BF16)

    chunks(lambda j, p: spread(j, p).wait_recv())
    scale = 1.0 / math.sqrt(D * ROWS * COLS * LANES)
    summed = total[...] * scale
    for a in range(3):
        turned = summed if a == 0 else pltpu.roll(summed, LANES - a * G, 1)
        for b in range(3):
            for c in range(3):
                out_weight[pl.ds(a * TAPS + (b * 3 + c) * O, O)] = turned[c * 96 + b * O : c * 96 + (b + 1) * O, :G]

    pl.when(inside(0, 1))(border_copy.wait_send)
    for copy, ok, _, _ in edge_copies:
        pl.when(ok)(copy.wait_send)
    pl.when(inside(1, 0))(down_copy.wait_send)
    pl.when(inside(-1, 0))(up_copy.wait_send)
    pl.when(inside(0, -1))(spill_copy.wait_send)
    chunks(lambda j, p: scatter(j, q, p).wait_send())

    @pl.when(is_owner)
    def _():
        others(DEEP, z, lambda p: across(z, p).wait_send())
        others(PLANE, q, lambda p: spread(mine, p).wait_send())


def shards(left_feat, right_feat, grad_out, conv_weight):
    vmem = pl.BlockSpec(memory_space=pltpu.VMEM)
    dma = pltpu.SemaphoreType.DMA
    weight = jnp.transpose(conv_weight, (2, 3, 4, 0, 1)).reshape(3, TAPS, G)
    padded = (D + 2) * G + 8
    wide_rows = lambda rows: pltpu.VMEM((rows, LANES), F32)
    half_rows = lambda rows: pltpu.VMEM((rows, LANES), BF16)
    grad_left, grad_right, grad_weight = pl.pallas_call(
        kernel,
        out_shape=(
            jax.ShapeDtypeStruct((C, LANES), BF16),
            jax.ShapeDtypeStruct((C, LANES), BF16),
            jax.ShapeDtypeStruct((3 * TAPS, G), F32),
        ),
        in_specs=[pl.BlockSpec(memory_space=pl.ANY)] * 4,
        out_specs=(vmem,) * 3,
        scratch_shapes=[
            half_rows(C), half_rows(C), half_rows(O * D), pltpu.VMEM((3, TAPS, G), BF16),
            wide_rows(O * D), half_rows(O * D), half_rows(O * D), half_rows(D * TAPS),
            wide_rows(padded), wide_rows(padded),
            wide_rows(C), wide_rows(C), wide_rows(C), wide_rows(C), wide_rows(C),
            wide_rows(C), half_rows(C), pltpu.VMEM((C, 2 * LANES), BF16), wide_rows(D * C), wide_rows(D * C),
            pltpu.VMEM((2 * LANES, 2 * LANES), BF16), wide_rows(96),
            pltpu.VMEM((2, O, LANES), BF16), pltpu.VMEM((2, 3, O, LANES), BF16),
            half_rows(HALF), half_rows(HALF), wide_rows(HALF), wide_rows(HALF),
            wide_rows(384), pltpu.VMEM((LANES, 384), F32), wide_rows(TAPS), wide_rows(TAPS),
            pltpu.VMEM((PLANE, CHUNK, LANES), F32), pltpu.VMEM((DEEP, CHUNK, LANES), F32),
            dma((4,)), dma((2,)), dma((2,)), dma((2, 3)), dma((2, 3)), dma((2,)), dma((2,)),
            dma((CHUNKS,)), dma((PLANE,)), dma((DEEP,)), dma((DEEP,)), dma((PLANE,)), dma((CHUNKS,)),
        ],
        compiler_params=pltpu.CompilerParams(
            collective_id=0, has_side_effects=True, vmem_limit_bytes=56 * 1024 * 1024
        ),
        cost_estimate=pl.CostEstimate(flops=10**9, bytes_accessed=4 * 10**6, transcendentals=0),
    )(
        left_feat.reshape(C, LANES),
        right_feat.reshape(C, LANES),
        grad_out.reshape(O * D, LANES),
        weight,
    )
    return (
        grad_left.reshape(C, 1, LANES),
        grad_right.reshape(C, 1, LANES),
        jnp.transpose(grad_weight.reshape(3, 3, 3, O, G), (3, 4, 0, 1, 2)),
    )


def solution(mesh):
    placed = (P(None, "rows", "cols"), P(None, "rows", "cols"), P(None, None, "rows", "cols"), P())
    return jax.shard_map(
        shards,
        mesh=mesh,
        in_specs=placed,
        out_specs=(P(None, "rows", "cols"), P(None, "rows", "cols"), P()),
        check_vma=False,
    )
```

```python
import functools
import math

import jax
import jax.numpy as jnp
from jax import lax
from jax.experimental import pallas as pl
from jax.experimental.pallas import tpu as pltpu
from jax.sharding import PartitionSpec as P

MESH = pl.DeviceIdType.MESH
F32, BF16 = jnp.float32, jnp.bfloat16
ROWS, COLS = 32, 16
D, G, O, C, LANES = 48, 40, 32, 320, 128
TAPS = 9 * O
PLANE, DEEP = 32, 16
CHUNKS, CHUNK = 18, 16
HALF = C // 2


def plane_device(q, z):
    if isinstance(q, int):
        return (lax.rem(z, 8) * 4 + q // 2 % 4, q // 8 * 4 + lax.div(z, 8) * 2 + q % 2)
    row = lax.rem(z, 8) * 4 + lax.rem(lax.div(q, 2), 4)
    return (row, lax.div(q, 8) * 4 + lax.div(z, 8) * 2 + lax.rem(q, 2))


def kernel(
    left_in, right_in, cot_in, weight_in, out_left, out_right, out_weight,
    left, right, cot, weight, wide, above, below, window, volume, grad_vol, left32, right32, gl32, gr32, spill32,
    by_tap, by_tap_bf, ext, moved_right, moved_left, near, edge32, edge_send, edges, border_send, border,
    spill_send, spill, mixed, weight_t, terms, total,
    part1, part2, s_in, s_row, r_row, s_edge, r_edge, s_one, r_one, s1, r1, s2, r2, s3, r3,
):
    row, col = lax.axis_index("rows"), lax.axis_index("cols")
    core = lax.rem(col, 2)
    q = (lax.div(col, 4) * 4 + lax.rem(row, 4)) * 2 + core
    z = lax.rem(lax.div(col, 2), 2) * 8 + lax.div(row, 4)
    is_owner = jnp.logical_or(core == 0, jnp.logical_or(q == 1, q == 17))
    mine = jnp.where(core == 0, lax.div(q, 2), jnp.where(q == 1, 16, 17))
    lane = lax.broadcasted_iota(jnp.int32, (8, LANES), 1)
    lane32 = lax.broadcasted_iota(jnp.int32, (O, LANES), 1)

    def inside(dr, dc):
        ok = None
        for pos, step, count in ((row, dr, ROWS), (col, dc, COLS)):
            if step:
                here = pos > 0 if step < 0 else pos < count - 1
                ok = here if ok is None else jnp.logical_and(ok, here)
        return ok

    around = [(dr, dc) for dr in (-1, 0, 1) for dc in (-1, 0, 1) if (dr, dc) != (0, 0)]

    gate = pltpu.get_barrier_semaphore()
    expected = PLANE + DEEP - 2

    def greet(device):
        pl.semaphore_signal(gate, inc=1, device_id=device, device_id_type=MESH)

    for dr, dc in around:
        ok = inside(dr, dc)
        expected = expected + ok.astype(jnp.int32)
        pl.when(ok)(functools.partial(greet, (row + dr, col + dc)))

    @pl.loop(0, PLANE)
    def _(p):
        pl.when(p != q)(functools.partial(greet, plane_device(p, z)))

    @pl.loop(0, DEEP)
    def _(p):
        pl.when(p != z)(functools.partial(greet, plane_device(q, p)))

    loads = [
        pltpu.make_async_copy(src, dst, s_in.at[i])
        for i, (src, dst) in enumerate(((right_in, right), (cot_in, cot), (left_in, left), (weight_in, weight)))
    ]
    for load in loads:
        load.start()

    def widen(src, dst, rows, step):
        @pl.loop(0, rows // step)
        def _(i):
            part = pl.ds(pl.multiple_of(i * step, step), step)
            dst[part] = src[part].astype(F32)

    loads[0].wait()
    widen(right, right32, C, 64)
    low, high = right32[pl.ds(0, HALF)], right32[pl.ds(HALF, HALF)]
    lane_half = lax.broadcasted_iota(jnp.int32, (HALF, LANES), 1)
    border_send[...] = jnp.where(lane_half >= 64, low, pltpu.roll(high, 64, 1)).astype(BF16)
    loads[1].wait()
    widen(cot, wide, O * D, 64)

    def edge_body(d, carry):
        first, last = carry
        t = wide[pl.ds(d, O, stride=D), :]
        first = jnp.where(lane32 == d, pltpu.roll(t, d, 1), first)
        last = jnp.where(lane32 == d, pltpu.roll(t, d + 1, 1), last)
        return first, last

    blank = jnp.zeros((O, LANES), F32)
    first, last = lax.fori_loop(0, D, edge_body, (blank, blank), unroll=4)
    edge_send[0] = last.astype(BF16)
    edge_send[1] = first.astype(BF16)

    pl.semaphore_wait(gate, expected)

    def remote(src, dst, send, recv, device):
        return pltpu.make_async_remote_copy(src, dst, send, recv, device_id=device, device_id_type=MESH)

    border_copy = remote(border_send, border, s_one.at[0], r_one.at[0], (row, col + 1))
    pl.when(inside(0, 1))(border_copy.start)
    edge_copies = []
    for side, dc in ((0, 1), (1, -1)):
        for dr in (-1, 0, 1):
            copy = remote(
                edge_send.at[side], edges.at[side, dr + 1],
                s_edge.at[side, dr + 1], r_edge.at[side, dr + 1], (row + dr, col + dc),
            )
            pl.when(inside(dr, dc))(copy.start)
            edge_copies.append((copy, inside(dr, dc), inside(-dr, -dc), edges.at[side, dr + 1]))
    down_copy = remote(cot_in, above, s_row.at[0], r_row.at[0], (row + 1, col))
    up_copy = remote(cot_in, below, s_row.at[1], r_row.at[1], (row - 1, col))
    pl.when(inside(1, 0))(down_copy.start)
    pl.when(inside(-1, 0))(up_copy.start)

    loads[2].wait()
    loads[3].wait()
    widen(left, left32, C, 64)
    for ref in (volume, grad_vol):
        ref[pl.ds(0, G)] = jnp.zeros((G, LANES), F32)
        ref[pl.ds((D + 1) * G, G + 8)] = jnp.zeros((G + 8, LANES), F32)

    @pl.loop(0, D)
    def _(d):
        grad_vol[pl.ds(pl.multiple_of((d + 1) * G, 8), G)] = jnp.zeros((G, LANES), F32)

    mixed[...] = jnp.zeros_like(mixed)
    weight_t[...] = jnp.zeros_like(weight_t)
    for a in range(3):
        for b in range(3):
            for c in range(3):
                mixed[pl.ds(c * 96 + b * O, O), pl.ds(0, G)] = weight[a, pl.ds((b * 3 + c) * O, O), :].astype(F32)
        weight_t[pl.ds(a * G, G)] = jnp.transpose(mixed[...])[:G]
    weights = weight_t[...][:, :TAPS].astype(BF16)
    terms[...] = jnp.zeros_like(terms)

    def settle(copy, ok, ref):
        pl.when(ok)(copy.wait_recv)

        @pl.when(jnp.logical_not(ok))
        def _():
            ref[...] = jnp.zeros_like(ref)

    def regroup(ref):
        return jnp.concatenate([ref[pl.ds(k, G, stride=8), :] for k in range(8)], axis=0)

    by_tap[...] = regroup(left32)
    by_tap_bf[...] = by_tap[...].astype(BF16)
    ext[:, pl.ds(LANES, LANES)] = regroup(right32).astype(BF16)
    source = lax.broadcasted_iota(jnp.int32, (2 * LANES, LANES), 0) - lax.broadcasted_iota(jnp.int32, (2 * LANES, LANES), 1)
    ring = source[:LANES]

    def pick(hit):
        return jnp.where(hit, 1.0, 0.0).astype(BF16)

    def turn_body(t, carry):
        d = t * 2
        rule = jnp.concatenate([pick(jnp.logical_or(ring == d + s, ring == d + s - LANES)) for s in range(2)], axis=1)
        turned = jnp.dot(by_tap_bf[...], rule, preferred_element_type=F32)
        for s in range(2):
            moved_left[pl.ds(pl.multiple_of((d + s) * C, 8), C)] = turned[:, s * LANES : (s + 1) * LANES]
        return carry

    lax.fori_loop(0, D // 2, turn_body, 0, unroll=8)

    def centre(b):
        def body(d, carry):
            base = pl.multiple_of(d * TAPS + 96 + b * O, 32)
            window[pl.ds(base, O)] = wide[pl.ds(d, O, stride=D), :].astype(BF16)
            return carry

        lax.fori_loop(0, D, body, 0, unroll=4)

    centre(1)
    for copy, _, ok, ref in edge_copies:
        settle(copy, ok, ref)
    for b in range(3):
        from_left, from_right = edges[0, b].astype(F32), edges[1, b].astype(F32)
        edge32[pl.ds(b * O, O)] = jnp.where(lane32 < 64, from_left, pltpu.roll(from_right, 64, 1))
    row_j = lax.broadcasted_iota(jnp.int32, (LANES, LANES), 0)
    col_w = lax.broadcasted_iota(jnp.int32, (LANES, LANES), 1)
    near[pl.ds(0, LANES), pl.ds(0, LANES)] = pick(row_j == col_w + 1)
    near[pl.ds(0, LANES), pl.ds(LANES, LANES)] = pick(row_j == col_w - 1)
    near[pl.ds(LANES, LANES), pl.ds(0, LANES)] = pick(jnp.logical_and(row_j >= 64, col_w == LANES - 1))
    near[pl.ds(LANES, LANES), pl.ds(LANES, LANES)] = pick(jnp.logical_and(row_j < 64, col_w == 0))
    lane96 = lax.broadcasted_iota(jnp.int32, (96, LANES), 1)

    def windows_body(t, carry):
        rows = []
        for s in range(4):
            d = t * 4 + s
            hit = jnp.logical_or(lane96 == d, lane96 == d + 64)
            rim = jnp.where(hit, edge32[...], 0.0).astype(BF16)
            rows.append(jnp.concatenate([window[pl.ds(pl.multiple_of(d * TAPS + 96, 32), 96)], rim], axis=1))
        sides = jnp.dot(jnp.concatenate(rows, axis=0), near[...], preferred_element_type=F32).astype(BF16)
        for s in range(4):
            d = t * 4 + s
            window[pl.ds(pl.multiple_of(d * TAPS, 32), 96)] = sides[s * 96 : (s + 1) * 96, :LANES]
            window[pl.ds(pl.multiple_of(d * TAPS + 192, 32), 96)] = sides[s * 96 : (s + 1) * 96, LANES:]
        return carry

    def rows_part():
        pl.when(inside(-1, 0))(down_copy.wait_recv)
        widen(above, wide, O * D, 64)
        centre(2)
        pl.when(inside(1, 0))(up_copy.wait_recv)
        widen(below, wide, O * D, 64)
        centre(0)
        lax.fori_loop(0, D // 4, windows_body, 0)

    @pl.when(row == 0)
    def _():
        above[...] = jnp.zeros_like(above)

    @pl.when(row == ROWS - 1)
    def _():
        below[...] = jnp.zeros_like(below)

    late = z >= 4
    pl.when(late)(rows_part)

    settle(border_copy, inside(0, -1), border)
    arrived = border[...].astype(F32)
    right32[pl.ds(0, HALF)] = arrived
    right32[pl.ds(HALF, HALF)] = pltpu.roll(arrived, 64, 1)
    ext[:, pl.ds(0, LANES)] = regroup(right32).astype(BF16)

    def volume_pair(t, carry):
        d = t * 2
        rule = jnp.concatenate([pick(source == LANES - d - s) for s in range(2)], axis=1)
        moved = jnp.dot(ext[...], rule, preferred_element_type=F32)
        for s in range(2):
            part = moved[:, s * LANES : (s + 1) * LANES]
            moved_right[pl.ds(pl.multiple_of((d + s) * C, 8), C)] = part
            slab = by_tap[pl.ds(0, G)] * part[:G]
            for k in range(1, 8):
                slab = slab + by_tap[pl.ds(k * G, G)] * part[k * G : (k + 1) * G]
            volume[pl.ds(pl.multiple_of((d + s + 1) * G, 8), G)] = slab * 0.125
        return carry

    lax.fori_loop(0, D // 2, volume_pair, 0, unroll=8)
    pl.when(jnp.logical_not(late))(rows_part)

    def block_of(d):
        return window[pl.ds(pl.multiple_of(d * TAPS, 32), TAPS)]

    def term_body(t, carry):
        lhs = jnp.concatenate([block_of(t * 4 + s) for s in range(4)], axis=1)
        rhs = jnp.concatenate(
            [volume[pl.ds(pl.multiple_of((t * 4 + s) * G, 8), LANES)].astype(BF16) for s in range(4)], axis=1
        )
        terms[...] += lax.dot_general(lhs, rhs, (((1,), (1,)), ((), ())), preferred_element_type=F32)
        return carry

    lax.fori_loop(0, D // 4, term_body, 0, unroll=6)

    def scatter(j, slot, p):
        return remote(terms.at[pl.ds(j * CHUNK, CHUNK)], part1.at[slot], s1.at[j], r1.at[slot], plane_device(p, z))

    def across(slot, p):
        return remote(part2.at[z], part2.at[slot], s2.at[p], r2.at[slot], plane_device(q, p))

    def spread(j, p):
        part = total.at[pl.ds(j * CHUNK, CHUNK)]
        return remote(part, part, s3.at[p], r3.at[j], plane_device(p, z))

    def others(count, me, what):
        for p in range(count):
            pl.when(p != me)(functools.partial(what, p))

    def chunks(what):
        for j in range(CHUNKS):
            p = 2 * j if j < 16 else (1, 17)[j - 16]
            pl.when(p != q)(functools.partial(what, j, p))

    chunks(lambda j, p: scatter(j, q, p).start())

    def volume_body(t, carry):
        rhs = jnp.concatenate([block_of(t * 2), block_of(t * 2 + 1)], axis=1)
        spread_ = jnp.dot(weights, rhs, preferred_element_type=F32)
        for s in range(2):
            part = pl.ds(pl.multiple_of((t * 2 + s) * G, 8), 3 * G)
            grad_vol[part] += spread_[: 3 * G, s * LANES : (s + 1) * LANES]
        return carry

    lax.fori_loop(0, D // 2, volume_body, 0, unroll=8)

    @pl.when(is_owner)
    def _():
        others(PLANE, q, lambda p: scatter(0, p, p).wait_recv())
        part1[q] = terms[pl.ds(pl.multiple_of(mine * CHUNK, CHUNK), CHUNK)]
        partial = part1[0]
        for p in range(1, PLANE):
            partial = partial + part1[p]
        part2[z] = partial
        others(DEEP, z, lambda p: across(z, p).start())

    @pl.loop(0, G // 8)
    def _(block):
        def level(d, carry):
            gl, gr, sp = carry
            inner = lane < LANES - d
            slab = grad_vol[pl.ds(pl.multiple_of((d + 1) * G + block * 8, 8), 8)]
            moved = pltpu.roll(slab, lax.rem(LANES - d, LANES), 1)
            here, there = jnp.where(inner, moved, 0.0), jnp.where(inner, 0.0, moved)
            at = [pl.ds(pl.multiple_of(d * C + k * G + block * 8, 8), 8) for k in range(8)]
            gl = [gl[k] + slab * moved_right[at[k]] for k in range(8)]
            turned = [moved_left[at[k]] for k in range(8)]
            gr = [gr[k] + here * turned[k] for k in range(8)]
            sp = [sp[k] + there * turned[k] for k in range(8)]
            return gl, gr, sp

        zeros = [jnp.zeros((8, LANES), F32)] * 8
        gl, gr, sp = lax.fori_loop(0, D, level, (zeros, zeros, zeros), unroll=16)
        for k in range(8):
            part = pl.ds(block * 64 + k, 8, stride=8)
            gl32[part, :] = gl[k] * 0.125
            gr32[part, :] = gr[k] * 0.125
            spill32[part, :] = sp[k] * 0.125

    spill_send[...] = jnp.where(lane_half >= 64, spill32[pl.ds(0, HALF)], pltpu.roll(spill32[pl.ds(HALF, HALF)], 64, 1))
    spill_copy = remote(spill_send, spill, s_one.at[1], r_one.at[1], (row, col - 1))
    pl.when(inside(0, -1))(spill_copy.start)

    @pl.when(is_owner)
    def _():
        others(DEEP, z, lambda p: across(p, p).wait_recv())
        whole = part2[0]
        for p in range(1, DEEP):
            whole = whole + part2[p]
        total[pl.ds(pl.multiple_of(mine * CHUNK, CHUNK), CHUNK)] = whole
        others(PLANE, q, lambda p: spread(mine, p).start())

    out_left[...] = gl32[...].astype(BF16)
    settle(spill_copy, inside(0, 1), spill)
    extra = spill[...]
    upper = lane_half >= LANES - (D - 1)
    out_right[pl.ds(0, HALF)] = (gr32[pl.ds(0, HALF)] + jnp.where(upper, extra, 0.0)).astype(BF16)
    out_right[pl.ds(HALF, HALF)] = (
        gr32[pl.ds(HALF, HALF)] + jnp.where(upper, pltpu.roll(extra, 64, 1), 0.0)
    ).astype(BF16)

    chunks(lambda j, p: spread(j, p).wait_recv())
    scale = 1.0 / math.sqrt(D * ROWS * COLS * LANES)
    summed = total[...] * scale
    for a in range(3):
        turned = summed if a == 0 else pltpu.roll(summed, LANES - a * G, 1)
        for b in range(3):
            for c in range(3):
                out_weight[pl.ds(a * TAPS + (b * 3 + c) * O, O)] = turned[c * 96 + b * O : c * 96 + (b + 1) * O, :G]

    pl.when(inside(0, 1))(border_copy.wait_send)
    for copy, ok, _, _ in edge_copies:
        pl.when(ok)(copy.wait_send)
    pl.when(inside(1, 0))(down_copy.wait_send)
    pl.when(inside(-1, 0))(up_copy.wait_send)
    pl.when(inside(0, -1))(spill_copy.wait_send)
    chunks(lambda j, p: scatter(j, q, p).wait_send())

    @pl.when(is_owner)
    def _():
        others(DEEP, z, lambda p: across(z, p).wait_send())
        others(PLANE, q, lambda p: spread(mine, p).wait_send())


def shards(left_feat, right_feat, grad_out, conv_weight):
    vmem = pl.BlockSpec(memory_space=pltpu.VMEM)
    dma = pltpu.SemaphoreType.DMA
    weight = jnp.transpose(conv_weight, (2, 3, 4, 0, 1)).reshape(3, TAPS, G)
    padded = (D + 2) * G + 8
    wide_rows = lambda rows: pltpu.VMEM((rows, LANES), F32)
    half_rows = lambda rows: pltpu.VMEM((rows, LANES), BF16)
    grad_left, grad_right, grad_weight = pl.pallas_call(
        kernel,
        out_shape=(
            jax.ShapeDtypeStruct((C, LANES), BF16),
            jax.ShapeDtypeStruct((C, LANES), BF16),
            jax.ShapeDtypeStruct((3 * TAPS, G), F32),
        ),
        in_specs=[pl.BlockSpec(memory_space=pl.ANY)] * 4,
        out_specs=(vmem,) * 3,
        scratch_shapes=[
            half_rows(C), half_rows(C), half_rows(O * D), pltpu.VMEM((3, TAPS, G), BF16),
            wide_rows(O * D), half_rows(O * D), half_rows(O * D), half_rows(D * TAPS),
            wide_rows(padded), wide_rows(padded),
            wide_rows(C), wide_rows(C), wide_rows(C), wide_rows(C), wide_rows(C),
            wide_rows(C), half_rows(C), pltpu.VMEM((C, 2 * LANES), BF16), wide_rows(D * C), wide_rows(D * C),
            pltpu.VMEM((2 * LANES, 2 * LANES), BF16), wide_rows(96),
            pltpu.VMEM((2, O, LANES), BF16), pltpu.VMEM((2, 3, O, LANES), BF16),
            half_rows(HALF), half_rows(HALF), wide_rows(HALF), wide_rows(HALF),
            wide_rows(384), pltpu.VMEM((LANES, 384), F32), wide_rows(TAPS), wide_rows(TAPS),
            pltpu.VMEM((PLANE, CHUNK, LANES), F32), pltpu.VMEM((DEEP, CHUNK, LANES), F32),
            dma((4,)), dma((2,)), dma((2,)), dma((2, 3)), dma((2, 3)), dma((2,)), dma((2,)),
            dma((CHUNKS,)), dma((PLANE,)), dma((DEEP,)), dma((DEEP,)), dma((PLANE,)), dma((CHUNKS,)),
        ],
        compiler_params=pltpu.CompilerParams(
            collective_id=0, has_side_effects=True, vmem_limit_bytes=56 * 1024 * 1024
        ),
        cost_estimate=pl.CostEstimate(flops=10**9, bytes_accessed=4 * 10**6, transcendentals=0),
    )(
        left_feat.reshape(C, LANES),
        right_feat.reshape(C, LANES),
        grad_out.reshape(O * D, LANES),
        weight,
    )
    return (
        grad_left.reshape(C, 1, LANES),
        grad_right.reshape(C, 1, LANES),
        jnp.transpose(grad_weight.reshape(3, 3, 3, O, G), (3, 4, 0, 1, 2)),
    )


def solution(mesh):
    placed = (P(None, "rows", "cols"), P(None, "rows", "cols"), P(None, None, "rows", "cols"), P())
    return jax.shard_map(
        shards,
        mesh=mesh,
        in_specs=placed,
        out_specs=(P(None, "rows", "cols"), P(None, "rows", "cols"), P()),
        check_vma=False,
    )
```
